32 devices in a mesh: fsdp: 2 (over x), heads: 4 (over z), tensor: 4 (over y, core).
Axes of the slice: x: 2, y: 2, z: 4, core: 2. Of those that a mesh axis runs over, the one named last changes fastest.
Arguments:
- latent_tokens: bfloat16 [16, 1024, 1152], P('fsdp', ('heads', 'tensor')), may hold values from -6 to 6
- labels: int32 [16], replicated, may hold values from 0 to 999
- timesteps: int32 [16], replicated, may hold values from 0 to 999
- class_table: bfloat16 [1000, 1152], P(None, 'fsdp'), may hold values from -6 to 6
- time_table: bfloat16 [1000, 1152], P(None, 'fsdp'), may hold values from -6 to 6
- ada_weight: bfloat16 [1152, 6912], P(('fsdp', 'heads'), 'tensor'), may hold values from -0.1875 to 0.1875
- ada_bias: bfloat16 [6912], P('tensor'), may hold values from -3 to 3
- qkv_weight: bfloat16 [1152, 3, 1152], P(('fsdp', 'heads'), None, 'tensor'), may hold values from -0.1875 to 0.1875
- qkv_bias: bfloat16 [3, 1152], P(None, 'tensor'), may hold values from -3 to 3
- proj_weight: bfloat16 [1152, 1152], P('tensor', ('fsdp', 'heads')), may hold values from -1.5 to 1.5
- proj_bias: bfloat16 [1152], replicated, may hold values from -3 to 3
- up_weight: bfloat16 [1152, 4608], P(('fsdp', 'heads'), 'tensor'), may hold values from -0.1875 to 0.1875
- up_bias: bfloat16 [4608], P('tensor'), may hold values from -3 to 3
- down_weight: bfloat16 [4608, 1152], P('tensor', ('fsdp', 'heads')), may hold values from -0.09375 to 0.09375
- down_bias: bfloat16 [1152], replicated, may hold values from -3 to 3
- cotangent: bfloat16 [16, 1024, 1152], P('fsdp', ('heads', 'tensor')), may hold values from -6 to 6
Outputs:
- block_out: bfloat16 [16, 1024, 1152], P('fsdp', ('heads', 'tensor'))
- grad_tokens: bfloat16 [16, 1024, 1152], P('fsdp', ('heads', 'tensor'))
- grad_class_table: float32 [1000, 1152], P(None, 'fsdp')
- grad_time_table: float32 [1000, 1152], P(None, 'fsdp')
- grad_ada_weight: float32 [1152, 6912], P(('fsdp', 'heads'), 'tensor')
- grad_ada_bias: float32 [6912], P('tensor')
- grad_qkv_weight: float32 [1152, 3, 1152], P(('fsdp', 'heads'), None, 'tensor')
- grad_qkv_bias: float32 [3, 1152], P(None, 'tensor')
- grad_proj_weight: float32 [1152, 1152], P('tensor', ('fsdp', 'heads'))
- grad_proj_bias: float32 [1152], replicated
- grad_up_weight: float32 [1152, 4608], P(('fsdp', 'heads'), 'tensor')
- grad_up_bias: float32 [4608], P('tensor')
- grad_down_weight: float32 [4608, 1152], P('tensor', ('fsdp', 'heads'))
- grad_down_bias: float32 [1152], replicated
The draws below stay inside these ranges and needn't reach their ends.
All inputs are finite; a program needn't handle non-finite values.
Results may differ from the reference program's by a relative error of at most 0.018.
The reference program's roundings to bfloat16 on the way count: a program that leaves them out, or rounds other values in their place, can miss the bound.
Values may be sent and summed in bfloat16 or wider, within the bound.
A program may use at most 192 MiB of HBM per device.

```python
import jax
import jax.numpy as jnp
from jax import lax

D = 1152
HEADS = 16
FF = 4608
NCLS = 1000
TSTEPS = 1000
SEQ = 1024
HEAD_DIM = 72
LATENTS = 16


def touch_ends(values, key, low, top_value):
    longest = values.shape.index(max(values.shape))
    spots = []
    for shift in (0, 1):
        where = [jax.random.randint(jax.random.fold_in(key, axis), (), 0, length) for axis, length in enumerate(values.shape)]
        where[longest] = (where[longest] + shift) % values.shape[longest]
        spots.append(tuple(where))
    return values.at[spots[0]].set(low).at[spots[1]].set(top_value)


def levels(rng, shape, cuts, least, top_value):
    loudness = 1.0
    for axis_at, parts in cuts:
        draws = jax.random.uniform(jax.random.fold_in(jax.random.fold_in(rng, 6), axis_at), (parts,), jnp.float32, least / len(cuts), top_value / len(cuts))
        loudness = loudness * jnp.repeat(jnp.exp(draws), shape[axis_at] // parts).reshape((-1,) + (1,) * (len(shape) - 1 - axis_at))
    return loudness


def gaussian(own_key, extent, scale, most, cuts=(), dtype=jnp.bfloat16):
    level = levels(own_key, extent, cuts, -0.22, 0.18) if cuts else 1.0
    drawn = jax.random.normal(own_key, extent, jnp.float32) * scale * level
    return jnp.minimum(jnp.maximum(drawn, -most), most).astype(dtype)


def setup_inputs(seed: int = 0) -> dict:
    key_list = jax.random.split(jax.random.key(seed), 17)
    latent_tokens = gaussian(key_list[0], (LATENTS, SEQ, D), 1.0, 6.0, ((0, 2), (1, 16)))
    labels = touch_ends(jax.random.randint(key_list[1], (LATENTS,), 0, NCLS), jax.random.fold_in(key_list[1], 1), 0, NCLS - 1).astype(jnp.int32)
    timesteps = touch_ends(jax.random.randint(key_list[2], (LATENTS,), 0, TSTEPS), jax.random.fold_in(key_list[2], 1), 0, TSTEPS - 1).astype(jnp.int32)
    class_table = gaussian(key_list[3], (NCLS, D), 1.0, 6.0, ((1, 2),))
    time_table = gaussian(key_list[4], (TSTEPS, D), 1.0, 6.0, ((1, 2),))
    ada_weight = gaussian(key_list[5], (D, 6 * D), D ** -0.5, 0.1875, ((0, 8), (1, 4)))
    ada_bias = gaussian(key_list[6], (6 * D,), 0.5, 3.0, ((0, 4),))
    qkv_weight = gaussian(key_list[7], (D, 3, D), D ** -0.5, 0.1875, ((0, 8), (2, 4)))
    qkv_bias = gaussian(key_list[8], (3, D), 0.5, 3.0, ((1, 4),))
    proj_weight = gaussian(key_list[9], (D, D), (max(D * 16 // SEQ, 1)) ** -0.5, 1.5, ((0, 4), (1, 8)))
    proj_bias = gaussian(key_list[10], (D,), 0.5, 3.0)
    up_weight = gaussian(key_list[11], (D, FF), D ** -0.5, 0.1875, ((0, 8), (1, 4)))
    up_bias = gaussian(key_list[12], (FF,), 0.5, 3.0, ((0, 4),))
    down_weight = gaussian(key_list[13], (FF, D), FF ** -0.5, 0.09375, ((0, 4), (1, 8)))
    down_bias = gaussian(key_list[14], (D,), 0.5, 3.0)
    cotangent = gaussian(key_list[15], (LATENTS, SEQ, D), 1.0, 6.0, ((0, 2), (1, 16)))
    return dict(latent_tokens=latent_tokens, labels=labels, timesteps=timesteps, class_table=class_table, time_table=time_table, ada_weight=ada_weight, ada_bias=ada_bias, qkv_weight=qkv_weight, qkv_bias=qkv_bias, proj_weight=proj_weight, proj_bias=proj_bias, up_weight=up_weight, up_bias=up_bias, down_weight=down_weight, down_bias=down_bias, cotangent=cotangent)


layer_eps = 1e-06

@jax.custom_vjp
def low(v):
    return lax.optimization_barrier(v.astype(jnp.bfloat16)).astype(jnp.float32)

@jax.custom_vjp
def reduced_backward(v):
    return v

def low_keep(v):
    return (low(v), None)

def low_pass(kept, grad):
    return (grad,)

def back_keep(v):
    return (v, None)

def back_low(kept, grad):
    return (low(grad),)
low.defvjp(low_keep, low_pass)
reduced_backward.defvjp(back_keep, back_low)

def matmul_result(formula, left, right):
    return jnp.einsum(formula, left, right, precision=lax.Precision.HIGHEST)

def norm_rows(values):
    centre = values - lax.optimization_barrier(jnp.mean(values, axis=-1, keepdims=True))
    spread = lax.optimization_barrier(jnp.mean(centre * centre, axis=-1, keepdims=True))
    return centre * lax.rsqrt(spread + layer_eps)

def attend_latent(block):
    factor = HEAD_DIM ** (-0.5)
    queries, keys_in, values_in = (block[:, 0], block[:, 1], block[:, 2])
    scores = reduced_backward(matmul_result('qhe,khe->hqk', queries, keys_in) * factor)
    probs = low(jax.nn.softmax(scores, axis=-1))
    return low(reduced_backward(matmul_result('hqk,khe->qhe', probs, values_in)))

def reference(latent_tokens, labels, timesteps, class_table, time_table, ada_weight, ada_bias, qkv_weight, qkv_bias, proj_weight, proj_bias, up_weight, up_bias, down_weight, down_bias, cotangent):

    def forward(tokens_in, class_rows, time_rows, ada_matrix, ada_offset, qkv_matrix, qkv_offset, projection_weight_local, projection_bias_local, up_weight_local, up_bias_local, down_weight_local, down_bias_local):
        condition = class_rows[labels] + time_rows[timesteps]
        lifted = low(jax.nn.silu(condition))
        modulation = reduced_backward(matmul_result('ld,dc->lc', lifted, ada_matrix) + ada_offset)
        pieces = [modulation[:, None, position * D:(position + 1) * D] for position in range(6)]
        shift_first, scale_first, gate_first, shift_second, scale_second, gate_second = pieces
        input_first = low(norm_rows(tokens_in) * (1.0 + scale_first) + shift_first)
        qkv_all = low(reduced_backward(matmul_result('lsd,dce->lsce', input_first, qkv_matrix) + qkv_offset))
        blocks = qkv_all.reshape(LATENTS, SEQ, 3, HEADS, HEAD_DIM)
        attention_output = lax.map(jax.checkpoint(attend_latent), blocks).reshape(LATENTS, SEQ, D)
        attention_branch = reduced_backward(matmul_result('tpz,zm->tpm', attention_output, projection_weight_local) + projection_bias_local)
        middle = tokens_in + gate_first * attention_branch
        feedforward_input = low(norm_rows(middle) * (1.0 + scale_second) + shift_second)
        preactivation = reduced_backward(matmul_result('vyg,gq->vyq', feedforward_input, up_weight_local) + up_bias_local)
        gelu_activations = low(jax.nn.gelu(preactivation, approximate=True))
        feedforward_branch = reduced_backward(matmul_result('tpz,zm->tpm', gelu_activations, down_weight_local) + down_bias_local)
        return middle + gate_second * feedforward_branch
    floats = tuple((member.astype(jnp.float32) for member in (latent_tokens, class_table, time_table, ada_weight, ada_bias, qkv_weight, qkv_bias, proj_weight, proj_bias, up_weight, up_bias, down_weight, down_bias)))
    block_out, pullback = jax.vjp(forward, *floats)
    gradients = pullback(cotangent.astype(jnp.float32))
    return (block_out.astype(jnp.bfloat16), gradients[0].astype(jnp.bfloat16), gradients[1], gradients[2], gradients[3], gradients[4], gradients[5], gradients[6], gradients[7], gradients[8], gradients[9], gradients[10], gradients[11], gradients[12])
```

```python
import jax
import jax.numpy as jnp
from jax import lax
from jax.sharding import PartitionSpec as P

HEAD_DIM = 72
GROUP = ("fsdp", "heads")


layer_eps = 1e-06


def norm_rows(values):
    centre = values - jnp.mean(values, axis=-1, keepdims=True)
    spread = jnp.mean(centre * centre, axis=-1, keepdims=True)
    return centre * lax.rsqrt(spread + layer_eps)


def gelu_tanh(values):
    return jax.nn.gelu(values, approximate=True)


def tensor_rows(values):
    return lax.all_gather(values, "tensor", axis=1, tiled=True)


def tensor_sums(values):
    return lax.psum_scatter(
        values.astype(jnp.bfloat16), "tensor", scatter_dimension=1, tiled=True
    ).astype(jnp.float32)


def to_owner(values):
    return lax.all_to_all(values, "heads", split_axis=0, concat_axis=1, tiled=True)


def to_tokens(values):
    return lax.all_to_all(values, "heads", split_axis=1, concat_axis=0, tiled=True)


def choose_rows(indices, count):
    return indices[:, None] == lax.broadcasted_iota(jnp.int32, (indices.shape[0], count), 1)


def attend_one(items):
    queries, keys_in, values_in = items
    factor = queries.shape[-1] ** (-0.5)
    scores = jnp.einsum("qe,ke->qk", queries, keys_in, preferred_element_type=jnp.float32) * factor
    highest = jnp.max(scores, axis=-1, keepdims=True)
    raised = jnp.exp(scores - highest)
    summed = jnp.sum(raised, axis=-1, keepdims=True)
    weights = (raised / summed).astype(jnp.bfloat16)
    result = jnp.einsum("qk,ke->qe", weights, values_in, preferred_element_type=jnp.float32)
    return (result.astype(jnp.bfloat16), (highest + jnp.log(summed))[..., 0])


def attend_back(items):
    queries, keys_in, values_in, log_total, grad_out = items
    factor = queries.shape[-1] ** (-0.5)
    scores = jnp.einsum("qe,ke->qk", queries, keys_in, preferred_element_type=jnp.float32) * factor
    probs = jnp.exp(scores - log_total[..., None])
    grad_values = jnp.einsum(
        "qk,qe->ke", probs.astype(jnp.bfloat16), grad_out, preferred_element_type=jnp.float32
    )
    grad_probs = jnp.einsum("qe,ke->qk", grad_out, values_in, preferred_element_type=jnp.float32)
    centred = jnp.sum(grad_probs * probs, axis=-1, keepdims=True)
    grad_scores = (probs * (grad_probs - centred)).astype(jnp.bfloat16)
    grad_queries = (
        jnp.einsum("qk,ke->qe", grad_scores, keys_in, preferred_element_type=jnp.float32) * factor
    )
    grad_keys = (
        jnp.einsum("qk,qe->ke", grad_scores, queries, preferred_element_type=jnp.float32) * factor
    )
    return tuple(v.astype(jnp.bfloat16) for v in (grad_queries, grad_keys, grad_values))


def product(formula, left, right):
    return jnp.einsum(formula, left, right, preferred_element_type=jnp.float32)


def owned_sum(values, dimension):
    return lax.psum_scatter(
        values.astype(jnp.bfloat16), GROUP, scatter_dimension=dimension, tiled=True
    ).astype(jnp.float32)


def shards(
    latent_tokens,
    labels,
    timesteps,
    class_table,
    time_table,
    ada_weight,
    ada_bias,
    qkv_weight,
    qkv_bias,
    proj_weight,
    proj_bias,
    up_weight,
    up_bias,
    down_weight,
    down_bias,
    cotangent,
):
    model_width = latent_tokens.shape[2]
    all_latents = labels.shape[0]
    head_rank = lax.axis_index("heads")
    tensor_size = lax.axis_size("tensor")
    head_size = lax.axis_size("heads")
    group_size = lax.axis_size("fsdp") * head_size
    own_latents = all_latents // group_size
    ada_rows, ada_columns = ada_weight.shape
    qkv_columns = qkv_bias.shape[1]
    up_columns = up_bias.shape[0]
    per_tensor = qkv_columns // HEAD_DIM

    qkv_whole = lax.all_gather(qkv_weight, GROUP, axis=0, tiled=True)
    residual_in = to_owner(latent_tokens).astype(jnp.float32)

    class_pick = choose_rows(labels, class_table.shape[0])
    time_pick = choose_rows(timesteps, time_table.shape[0])
    condition = product("ac,cd->ad", class_pick.astype(jnp.bfloat16), class_table) + product(
        "ac,cd->ad", time_pick.astype(jnp.bfloat16), time_table
    )
    lifted_wide, silu_back = jax.vjp(jax.nn.silu, condition)
    lifted = lax.dynamic_slice_in_dim(lifted_wide, head_rank * ada_rows, ada_rows, 1).astype(
        jnp.bfloat16
    )
    ada_part = product("ar,rc->ac", lifted, ada_weight)
    ada_part = lax.all_to_all(ada_part, GROUP, split_axis=0, concat_axis=0, tiled=True)
    ada_own = jnp.sum(ada_part.reshape(group_size, own_latents, ada_columns), axis=0) + ada_bias
    modulation = lax.all_gather(ada_own, "tensor", axis=1, tiled=True)
    pieces = [
        modulation[:, None, position * model_width : (position + 1) * model_width]
        for position in range(6)
    ]
    shift_first, scale_first, gate_first, shift_second, scale_second, gate_second = pieces

    normed_first, norm_back_first = jax.vjp(norm_rows, residual_in)
    input_first = (normed_first * (1.0 + scale_first) + shift_first).astype(jnp.bfloat16)
    rows_first = tensor_rows(input_first)
    sequence = rows_first.shape[1]
    proj_whole = lax.all_gather(proj_weight, GROUP, axis=1, tiled=True)
    up_whole = lax.all_gather(up_weight, GROUP, axis=0, tiled=True)
    down_whole = lax.all_gather(down_weight, GROUP, axis=1, tiled=True)

    def split_heads(values):
        cut = values.reshape(own_latents, sequence, per_tensor, HEAD_DIM)
        return cut.transpose(0, 2, 1, 3).reshape(own_latents * per_tensor, sequence, HEAD_DIM)

    def join_heads(values):
        cut = values.reshape(own_latents, per_tensor, sequence, HEAD_DIM)
        return cut.transpose(0, 2, 1, 3).reshape(own_latents, sequence, qkv_columns)

    qkv_local = (product("lsd,dce->lsce", rows_first, qkv_whole) + qkv_bias).astype(jnp.bfloat16)
    queries, keys_in, values_in = (split_heads(qkv_local[:, :, index]) for index in range(3))
    attention_output, log_total = lax.map(attend_one, (queries, keys_in, values_in))
    mixed = join_heads(attention_output)
    attention_branch = tensor_sums(product("tpz,zm->tpm", mixed, proj_whole)) + proj_bias
    middle = residual_in + gate_first * attention_branch
    normed_second, norm_back_second = jax.vjp(norm_rows, middle)
    input_second = (normed_second * (1.0 + scale_second) + shift_second).astype(jnp.bfloat16)
    rows_second = tensor_rows(input_second)
    preactivation = product("vyg,gq->vyq", rows_second, up_whole) + up_bias
    activated_wide, gelu_back = jax.vjp(gelu_tanh, preactivation)
    activated = activated_wide.astype(jnp.bfloat16)
    feedforward_branch = tensor_sums(product("tpz,zm->tpm", activated, down_whole)) + down_bias
    block_out = to_tokens((middle + gate_second * feedforward_branch).astype(jnp.bfloat16))

    grad_out = to_owner(cotangent).astype(jnp.float32)
    grad_branch_second = (grad_out * gate_second).astype(jnp.bfloat16)
    gate_second_sum = jnp.sum(grad_out * feedforward_branch, axis=1)
    second_rows = tensor_rows(grad_branch_second)
    down_owned = owned_sum(product("egr,egh->rh", activated, second_rows), 1)
    grad_act = product("xjw,mw->xjm", second_rows, down_whole)
    grad_preactivation = gelu_back(grad_act)[0].astype(jnp.bfloat16)
    up_owned = owned_sum(product("box,bor->xr", rows_second, grad_preactivation), 0)
    grad_input_second = tensor_sums(product("rqt,xt->rqx", grad_preactivation, up_whole))
    shift_second_sum = jnp.sum(grad_input_second, axis=1)
    scale_second_sum = jnp.sum(grad_input_second * normed_second, axis=1)
    grad_middle = grad_out + norm_back_second(grad_input_second * (1.0 + scale_second))[0]
    grad_branch_first = (grad_middle * gate_first).astype(jnp.bfloat16)
    gate_first_sum = jnp.sum(grad_middle * attention_branch, axis=1)
    first_rows = tensor_rows(grad_branch_first)
    proj_owned = owned_sum(product("egr,egh->rh", mixed, first_rows), 1)
    grad_mixed = split_heads(product("xjw,mw->xjm", first_rows, proj_whole).astype(jnp.bfloat16))
    grad_heads = lax.map(attend_back, (queries, keys_in, values_in, log_total, grad_mixed))
    grad_qkv = jnp.stack([join_heads(values) for values in grad_heads], axis=2)
    qkv_owned = owned_sum(product("lsd,lsce->dce", rows_first, grad_qkv), 0)
    grad_input_first = tensor_sums(product("lsce,dce->lsd", grad_qkv, qkv_whole))
    shift_first_sum = jnp.sum(grad_input_first, axis=1)
    scale_first_sum = jnp.sum(grad_input_first * normed_first, axis=1)
    grad_tokens = to_tokens(
        (grad_middle + norm_back_first(grad_input_first * (1.0 + scale_first))[0]).astype(
            jnp.bfloat16
        )
    )

    modul_part = jnp.concatenate(
        [
            shift_first_sum,
            scale_first_sum,
            gate_first_sum,
            shift_second_sum,
            scale_second_sum,
            gate_second_sum,
        ],
        axis=1,
    ).reshape(own_latents, tensor_size, ada_columns)
    modul_part = lax.all_to_all(modul_part, "tensor", split_axis=1, concat_axis=1, tiled=True)
    modul_own = jnp.sum(modul_part, axis=1).astype(jnp.bfloat16)
    modul_grad = lax.all_gather(modul_own, GROUP, axis=0, tiled=True)
    ada_grad = product("ar,ac->rc", lifted, modul_grad)
    ada_bias_grad = jnp.sum(modul_grad.astype(jnp.float32), axis=0)
    lifted_grad = lax.all_gather(
        product("ac,rc->ar", modul_grad, ada_weight), ("heads", "tensor"), axis=0
    )
    lifted_grad = jnp.sum(lifted_grad.reshape(head_size, tensor_size, all_latents, ada_rows), axis=1)
    lifted_grad = lifted_grad.transpose(1, 0, 2).reshape(all_latents, head_size * ada_rows)
    cond_columns = silu_back(lifted_grad)[0]
    class_grad = jnp.dot(
        class_pick.astype(jnp.float32).T, cond_columns, precision=lax.Precision.HIGHEST
    )
    time_grad = jnp.dot(
        time_pick.astype(jnp.float32).T, cond_columns, precision=lax.Precision.HIGHEST
    )

    bias_part = jnp.concatenate(
        [
            jnp.sum(grad_qkv.astype(jnp.float32), axis=(0, 1)).reshape(-1),
            jnp.sum(grad_preactivation.astype(jnp.float32), axis=(0, 1)),
            jnp.sum(first_rows.astype(jnp.float32), axis=(0, 1)),
            jnp.sum(second_rows.astype(jnp.float32), axis=(0, 1)),
        ]
    )
    bias_part = jnp.pad(bias_part, (0, -bias_part.shape[0] % 1024)).reshape(1, -1, 128)
    bias_sums = jnp.sum(lax.all_gather(bias_part, GROUP, axis=0, tiled=True), axis=0).reshape(-1)
    first_cut = 3 * qkv_columns
    second_cut = first_cut + up_columns
    third_cut = second_cut + model_width
    return (
        block_out,
        grad_tokens,
        class_grad,
        time_grad,
        ada_grad,
        ada_bias_grad,
        qkv_owned,
        bias_sums[:first_cut].reshape(3, qkv_columns),
        proj_owned,
        bias_sums[second_cut:third_cut],
        up_owned,
        bias_sums[first_cut:second_cut],
        down_owned,
        bias_sums[third_cut : third_cut + model_width],
    )


def solution(mesh):
    in_specs = (
        P("fsdp", ("heads", "tensor"), None),
        P(),
        P(),
        P(None, "fsdp"),
        P(None, "fsdp"),
        P(("fsdp", "heads"), "tensor"),
        P("tensor"),
        P(("fsdp", "heads"), None, "tensor"),
        P(None, "tensor"),
        P("tensor", ("fsdp", "heads")),
        P(),
        P(("fsdp", "heads"), "tensor"),
        P("tensor"),
        P("tensor", ("fsdp", "heads")),
        P(),
        P("fsdp", ("heads", "tensor"), None),
    )
    out_specs = (
        P("fsdp", ("heads", "tensor"), None),
        P("fsdp", ("heads", "tensor"), None),
        P(None, "fsdp"),
        P(None, "fsdp"),
        P(("fsdp", "heads"), "tensor"),
        P("tensor"),
        P(("fsdp", "heads"), None, "tensor"),
        P(None, "tensor"),
        P("tensor", ("fsdp", "heads")),
        P(),
        P(("fsdp", "heads"), "tensor"),
        P("tensor"),
        P("tensor", ("fsdp", "heads")),
        P(),
    )
    return jax.shard_map(shards, mesh=mesh, in_specs=in_specs, out_specs=out_specs, check_vma=False)
```
